512 devices in a mesh: dp: 8 (over z_lo), mp: 64 (over z_hi, y, x, core).
Axes of the slice: x: 4, y: 4, z: 16 (z_hi: 2, z_lo: 8; z = z_hi * 8 + z_lo), core: 2. Of those that a mesh axis runs over, the one named last changes fastest.
Arguments:
- narrow_input: bfloat16 [25088, 320], P(('dp', 'mp')), may hold values from 0 to 2
- narrow_output: bfloat16 [25088, 320], P(('dp', 'mp')), may hold values from 0 to 2
- narrow_mask: int32 [25088, 320], P(('dp', 'mp')), may hold values 0 or 1
- wide_cotangent: bfloat16 [32, 14, 14, 2560], P('dp', None, None, 'mp'), may hold values from -6 to 6
- wide_mask: int32 [32, 14, 14, 2560], P('dp', None, None, 'mp'), may hold values 0 or 1
- narrow_weight: bfloat16 [3, 3, 320, 320], replicated, may hold values from -0.109375 to 0.109375
- wide_weight: bfloat16 [3, 3, 1280, 2560], P(None, None, None, 'mp'), may hold values from -0.0546875 to 0.0546875
Outputs:
- narrow_gradient: bfloat16 [3, 3, 320, 320], replicated
- wide_gradient: bfloat16 [3, 3, 1280, 2560], P(None, None, 'dp', 'mp')
- input_gradient: bfloat16 [25088, 320], P(('dp', 'mp'))
The draws below stay inside these ranges and needn't reach their ends.
All inputs are finite; a program needn't handle non-finite values. No bound on the sum of `narrow_mask` or of `wide_mask` on one device may be relied on, other than what follows from the above.
Results may differ from the reference program's by a relative error of at most 0.012.
Values may be sent and summed in bfloat16 or wider, within the bound.
A program may use at most 128 MiB of HBM per device.

```python
import jax
import jax.numpy as jnp
from jax import lax

C = 320
COUT = 2560
HN = 28
IMG_DP = 4
HW = 14
CW = 1280
NIMG = 32
NPIX = 25088
N_DP = 8


def plant(array, key, smallest, top_value):
    spot = [jax.random.randint(jax.random.fold_in(key, axis), (), 0, length) for axis, length in enumerate(array.shape)]
    longest = array.shape.index(max(array.shape))
    neighbour = spot[:longest] + [(spot[longest] + 1) % array.shape[longest]] + spot[longest + 1:]
    return array.at[tuple(spot)].set(smallest).at[tuple(neighbour)].set(top_value)


def block_levels(rng, dims, shards, smallest, top_value):
    level = 1.0
    for axis_at, blocks in shards:
        draws = jax.random.uniform(jax.random.fold_in(jax.random.fold_in(rng, 6), axis_at), (blocks,), jnp.float32, smallest / len(shards), top_value / len(shards))
        level = level * jnp.repeat(jnp.exp(draws), dims[axis_at] // blocks).reshape((-1,) + (1,) * (len(dims) - 1 - axis_at))
    return level


def bell_draw(own_key, shape, width, most, shards=(), held_as=jnp.bfloat16):
    drawn = jax.random.normal(own_key, shape, jnp.float32) * width
    if len(shards) > 0:
        drawn = block_levels(own_key, shape, shards, -0.22, 0.18) * drawn
    return jnp.clip(drawn, min=-most, max=most).astype(held_as)


def setup_inputs(seed: int = 0) -> dict:
    key_list = jax.random.split(jax.random.key(seed), 8)
    narrow_input = jnp.clip(2.0 * jax.random.uniform(key_list[0], (NPIX, C), jnp.float32) ** block_levels(key_list[0], (NPIX, C), ((0, 512),), -0.2, 0.2), 0.0, 2.0).astype(jnp.bfloat16)
    narrow_output = jnp.clip(2.0 * jax.random.uniform(key_list[1], (NPIX, C), jnp.float32) ** block_levels(key_list[1], (NPIX, C), ((0, 512),), -0.2, 0.2), 0.0, 2.0).astype(jnp.bfloat16)
    narrow_mask = plant((jax.random.randint(key_list[2], (NPIX, C), 0, 2) < 1).astype(jnp.int32), jax.random.fold_in(key_list[2], 1), 0, 1)
    wide_cotangent = bell_draw(key_list[3], (NIMG, HW, HW, COUT), 1.0, 6.0, ((0, 8), (3, 64)))
    wide_mask = plant((jax.random.randint(key_list[4], (NIMG, HW, HW, COUT), 0, 2) < 1).astype(jnp.int32), jax.random.fold_in(key_list[4], 1), 0, 1)
    narrow_weight = bell_draw(key_list[5], (3, 3, C, C), (9 * C) ** -0.5, 0.109375)
    wide_weight = bell_draw(key_list[6], (3, 3, CW, COUT), (9 * CW) ** -0.5, 0.0546875, ((3, 64),))
    return {"narrow_input": narrow_input, "narrow_output": narrow_output, "narrow_mask": narrow_mask, "wide_cotangent": wide_cotangent, "wide_mask": wide_mask, "narrow_weight": narrow_weight, "wide_weight": wide_weight}


def to_coarse(images):
    count, rows, cols, chans = images.shape
    grid = images.reshape(count, rows // 2, 2, cols // 2, 2, chans)
    return grid.transpose(0, 1, 3, 2, 4, 5).reshape(count, rows // 2, cols // 2, 4 * chans)


def to_fine(coarse):
    count, rows, cols, chans = coarse.shape
    grid = coarse.reshape(count, rows, cols, 2, 2, chans // 4)
    return grid.transpose(0, 1, 3, 2, 4, 5).reshape(count, 2 * rows, 2 * cols, chans // 4)


def pad_grid(images):
    return jnp.pad(images, ((0, 0), (1, 1), (1, 1), (0, 0)))


def reference(narrow_input, narrow_output, narrow_mask, wide_cotangent, wide_mask, narrow_weight, wide_weight):
    total_images = IMG_DP * N_DP
    offset_rows = HN * HN // 2
    input_std = jnp.roll(narrow_input, offset_rows, 0)
    output_std = jnp.roll(narrow_output, offset_rows, 0)
    mask_std = jnp.roll(narrow_mask, offset_rows, 0)
    wide_in = to_coarse(output_std.reshape(total_images, HN, HN, C))
    wide_tangent = wide_cotangent * wide_mask.astype(jnp.bfloat16)
    padded_in = pad_grid(wide_in)
    padded_tan = pad_grid(wide_tangent)

    def group_sum(carry, group):
        start = (group * IMG_DP).astype(jnp.int32)
        block_in = lax.dynamic_slice_in_dim(padded_in, start, IMG_DP, 0)
        block_tan = lax.dynamic_slice_in_dim(wide_tangent, start, IMG_DP, 0).reshape(-1, COUT)
        terms = []
        for tap_row in range(3):
            for tap_col in range(3):
                source = block_in[:, tap_row:tap_row + HW, tap_col:tap_col + HW, :].reshape(-1, CW)
                terms.append(jnp.dot(source.T, block_tan, preferred_element_type=jnp.float32))
        part = jnp.stack(terms).reshape(3, 3, CW, COUT)
        part = lax.optimization_barrier(part.astype(jnp.bfloat16)).astype(jnp.float32)
        return carry + part, None

    groups = jnp.arange(N_DP, dtype=jnp.int32)
    wide_total, unused = lax.scan(group_sum, jnp.zeros((3, 3, CW, COUT), jnp.float32), groups)
    wide_gradient = (wide_total / total_images).astype(jnp.bfloat16)

    wide_back = jnp.zeros((total_images * HW * HW, CW), jnp.float32)
    for tap_row in range(3):
        for tap_col in range(3):
            moved = padded_tan[:, 2 - tap_row:2 - tap_row + HW, 2 - tap_col:2 - tap_col + HW, :].reshape(-1, COUT)
            wide_back = wide_back + jnp.dot(moved, wide_weight[tap_row, tap_col].T, preferred_element_type=jnp.float32)
    narrow_back = to_fine(wide_back.reshape(total_images, HW, HW, CW)).reshape(-1, C).astype(jnp.bfloat16)
    narrow_tangent = narrow_back * mask_std.astype(jnp.bfloat16)

    input_pad = pad_grid(input_std.reshape(total_images, HN, HN, C))
    tangent_pad = pad_grid(narrow_tangent.reshape(total_images, HN, HN, C))
    narrow_terms = []
    input_gradient = jnp.zeros((total_images * HN * HN, C), jnp.float32)
    for tap_row in range(3):
        for tap_col in range(3):
            source = input_pad[:, tap_row:tap_row + HN, tap_col:tap_col + HN, :].reshape(-1, C)
            narrow_terms.append(jnp.dot(source.T, narrow_tangent, preferred_element_type=jnp.float32))
            moved = tangent_pad[:, 2 - tap_row:2 - tap_row + HN, 2 - tap_col:2 - tap_col + HN, :].reshape(-1, C)
            input_gradient = input_gradient + jnp.dot(moved, narrow_weight[tap_row, tap_col].T, preferred_element_type=jnp.float32)
    narrow_total = jnp.stack(narrow_terms).reshape(3, 3, C, C)
    narrow_gradient = (narrow_total / total_images).astype(jnp.bfloat16)
    input_gradient = jnp.roll(input_gradient.astype(jnp.bfloat16), -offset_rows, 0)
    return narrow_gradient, wide_gradient, input_gradient
```

```python
import functools

import jax
import jax.numpy as jnp
import numpy as np
from jax import lax
from jax.experimental import pallas as pl
from jax.experimental.pallas import tpu as pltpu
from jax.sharding import PartitionSpec as P

BF = jnp.bfloat16
F32 = jnp.float32
MESH = pl.DeviceIdType.MESH
PLANE = [(dy, dx) for dy in range(4) for dx in range(4) if (dy, dx) != (0, 0)]
VMEM_BYTES = 48 * 1024 * 1024


def place():
    g = lax.axis_index("dp")
    m = lax.axis_index("mp")
    return g, m // 32, (m // 8) % 4, (m // 2) % 4, m % 2


def device(g, zh, y, x, c):
    return (g, ((zh * 4 + y) * 4 + x) * 2 + c)


def remote(src, dst, send_sem, recv_sem, target):
    return pltpu.make_async_remote_copy(
        src_ref=src,
        dst_ref=dst,
        send_sem=send_sem,
        recv_sem=recv_sem,
        device_id=target,
        device_id_type=MESH,
    )


def greet(barrier, target):
    pl.semaphore_signal(barrier, inc=1, device_id=target, device_id_type=MESH)


def mm(left, right):
    return jnp.dot(left, right, preferred_element_type=F32)


def row_member(g, zh, y, x, c, d):
    other = (2 * x + c + d) % 8
    return device(g, zh, y, other // 2, other % 2)


def coarse_from_fine():
    out = np.zeros((4, 128, 512), np.float32)
    for i in range(2):
        for j in range(2):
            for p in range(7):
                for q in range(14):
                    fine = (2 * p + i) * 28 + 2 * q + j
                    out[2 * i + j, p * 14 + q, (fine // 49) * 64 + fine % 49] = 1
    return out


def fine_from_coarse():
    out = np.zeros((448, 512), np.float32)
    for i in range(2):
        for j in range(2):
            for p in range(7):
                for q in range(14):
                    fine = (2 * p + i) * 28 + 2 * q + j
                    out[28 + fine, (2 * i + j) * 128 + p * 14 + q] = 1
            for q in range(14):
                spot = (2 * i + j) * 128 + 98 + q
                out[(0 if i == 1 else 420) + 2 * q + j, spot] = 1
    return out


def spread():
    out = np.zeros((2, 320, 640), np.float32)
    for k in range(320):
        out[0, k, k] = 1
        out[1, k, 320 + k] = 1
    return out


def gather_kernel(
    blk, perm, put, gath, halo, xall, mine, pair, row_s, row_r, halo_s, halo_r, z_s, z_r, pl_s, pl_r, co_s, co_r
):
    g, zh, y, x, c = place()
    j = 2 * x + c
    row = (g * 8 + zh * 4 + y) % 64
    odd = y % 2
    is13 = (zh == 1) & (y == 3)
    is03 = (zh == 0) & (y == 3)
    barrier = pltpu.get_barrier_semaphore()

    gives = jnp.where(odd == 0, j == 0, j == 7)
    near = (row + jnp.where(odd == 0, 63, 1)) % 64
    near_g, near_zh, near_y = near // 8, (near // 4) % 2, near % 4
    near_j = jnp.where(odd == 0, 7, 0)
    halo_source = device(near_g, near_zh, near_y, near_j // 2, near_j % 2)

    for d in range(1, 8):
        greet(barrier, row_member(g, zh, y, x, c, d))
    greet(barrier, halo_source)
    for dy, dx in PLANE:
        if dy != 0:
            greet(barrier, device(g, zh, (y + dy) % 4, (x + dx) % 4, c))
    greet(barrier, device(jnp.where(is03, (g + 7) % 8, g), 1 - zh, y, x, c))

    @pl.when(is13)
    def _():
        greet(barrier, device((g + 7) % 8, 1, 3, x, c))

    total = 7 + 12 + 1 + jnp.where(gives, 8, 0) + jnp.where(is13, 1, 0)
    pl.semaphore_wait(barrier, total)

    gath[j] = blk[...]
    row_copies = []
    for d in range(1, 8):
        copy = remote(blk, gath.at[j], row_s.at[d - 1], row_r.at[d - 1], row_member(g, zh, y, x, c, d))
        copy.start()
        row_copies.append(copy)

    def halo_copy(d):
        return remote(blk.at[1], halo, halo_s.at[d], halo_r, device(near_g, near_zh, near_y, d // 2, d % 2))

    @pl.when(gives)
    def _():
        for d in range(8):
            halo_copy(d).start()

    for copy in row_copies:
        copy.wait()

    part = jnp.zeros((32, 640), F32)
    for jj in range(2):
        acc = jnp.zeros((32, 320), F32)
        for b in range(8):
            sel = perm[2 * c + jj, pl.ds(pl.multiple_of(32 * x, 32), 32), 64 * b : 64 * b + 64]
            acc = acc + mm(sel, gath[b, 0])
        part = part + mm(acc.astype(BF), put[jj])
    mine[...] = part.astype(BF)

    z_a = remote(
        mine, pair.at[zh], z_s.at[0], z_r.at[0], device(jnp.where(is13, (g + 1) % 8, g), 1 - zh, y, x, c)
    )
    z_b = remote(mine, pair.at[1], z_s.at[1], z_r.at[1], device((g + 1) % 8, 1, 3, x, c))
    z_a.start()

    @pl.when(is13)
    def _():
        z_b.start()

    @pl.when(jnp.logical_not(is13))
    def _():
        pair[zh] = mine[...]

    z_a.wait()

    @pl.when(is13)
    def _():
        z_b.wait()

    xall[c, y, x] = pair[...]
    plane_copies = []
    for k, (dy, dx) in enumerate(PLANE):
        copy = remote(
            pair, xall.at[c, y, x], pl_s.at[k], pl_r.at[k], device(g, zh, (y + dy) % 4, (x + dx) % 4, c)
        )
        copy.start()
        plane_copies.append(copy)
    peer = device(g, zh, y, x, 1 - c)
    core_copies = []
    for k, (dy, dx) in enumerate([(0, 0)] + PLANE):
        if k > 0:
            plane_copies[k - 1].wait_recv()
        spot = xall.at[c, (y + 4 - dy) % 4, (x + 4 - dx) % 4]
        copy = remote(spot, spot, co_s.at[k], co_r.at[k], peer)
        copy.start()
        core_copies.append(copy)
    for copy in plane_copies:
        copy.wait_send()
    for copy in core_copies:
        copy.wait()
    halo_copy(0).wait_recv()

    @pl.when(gives)
    def _():
        for d in range(8):
            halo_copy(d).wait_send()


def gather_call(blk):
    vm = pl.BlockSpec(memory_space=pltpu.VMEM)
    return pl.pallas_call(
        gather_kernel,
        out_shape=(
            jax.ShapeDtypeStruct((8, 3, 64, 320), BF),
            jax.ShapeDtypeStruct((64, 320), BF),
            jax.ShapeDtypeStruct((2, 4, 4, 2, 32, 640), BF),
        ),
        in_specs=[vm] * 3,
        out_specs=(vm, vm, vm),
        scratch_shapes=[
            pltpu.VMEM((32, 640), BF),
            pltpu.VMEM((2, 32, 640), BF),
            pltpu.SemaphoreType.DMA((7,)),
            pltpu.SemaphoreType.DMA((7,)),
            pltpu.SemaphoreType.DMA((8,)),
            pltpu.SemaphoreType.DMA,
            pltpu.SemaphoreType.DMA((2,)),
            pltpu.SemaphoreType.DMA((2,)),
            pltpu.SemaphoreType.DMA((15,)),
            pltpu.SemaphoreType.DMA((15,)),
            pltpu.SemaphoreType.DMA((16,)),
            pltpu.SemaphoreType.DMA((16,)),
        ],
        compiler_params=pltpu.CompilerParams(
            collective_id=0, has_side_effects=True, vmem_limit_bytes=VMEM_BYTES
        ),
        name="gather_rows",
    )(blk, jnp.asarray(coarse_from_fine(), BF), jnp.asarray(spread(), BF))


def reduce_kernel(
    tcol, w, nb, psend, precv, part, rbuf, acc, zsend, zrecv, co_s, co_r, pl_s, pl_r, z_s, z_r, row_s, row_r
):
    g, zh, y, x, c = place()
    is13 = (zh == 1) & (y == 3)
    is03 = (zh == 0) & (y == 3)
    peer = device(g, zh, y, x, 1 - c)
    barrier = pltpu.get_barrier_semaphore()
    for d in range(1, 8):
        greet(barrier, row_member(g, zh, y, x, c, d))
    for dy, dx in PLANE:
        if dy != 0:
            greet(barrier, device(g, zh, (y + dy) % 4, (x + dx) % 4, c))
    greet(barrier, device(jnp.where(is13, (g + 1) % 8, g), 1 - zh, y, x, c))

    @pl.when(is13)
    def _():
        greet(barrier, device((g + 1) % 8, 1, 3, x, c))

    pl.semaphore_wait(barrier, 7 + 12 + 1 + jnp.where(is13, 1, 0))

    theirs = pl.ds(pl.multiple_of((1 - c) * 640, 128), 640)
    ours = pl.ds(pl.multiple_of(c * 640, 128), 640)
    core_copies = []
    for dy in (1, 2, 3, 0):
        yy = (y + dy) % 4
        psend[yy] = mm(tcol[yy], w[:, theirs]).astype(BF)
        copy = remote(psend.at[yy], precv.at[yy], co_s.at[dy], co_r.at[dy], peer)
        copy.start()
        core_copies.append(copy)
    plane_copies = []
    for n, dy in enumerate((1, 2, 3, 0)):
        yy = (y + dy) % 4
        own = mm(tcol[yy], w[:, ours])
        core_copies[n].wait_recv()
        part[yy] = (own + precv[yy].astype(F32)).astype(BF).reshape(4, 2, 32, 640)
        for dx in range(4):
            if (dy, dx) == (0, 0):
                continue
            k = PLANE.index((dy, dx))
            xx = (x + dx) % 4
            copy = remote(part.at[yy, xx], rbuf.at[k], pl_s.at[k], pl_r.at[k], device(g, zh, yy, xx, c))
            copy.start()
            plane_copies.append((k, copy))
    acc[...] = part[y, x].astype(F32)
    for k, copy in plane_copies:
        copy.wait_recv()
        acc[...] += rbuf[k].astype(F32)
    zsend[...] = acc[...].astype(BF)
    z_a = remote(
        zsend.at[1 - zh],
        zrecv.at[zh],
        z_s.at[0],
        z_r.at[0],
        device(jnp.where(is03, (g + 7) % 8, g), 1 - zh, y, x, c),
    )
    z_b = remote(zsend.at[1], zrecv.at[1], z_s.at[1], z_r.at[1], device((g + 7) % 8, 1, 3, x, c))
    z_a.start()

    @pl.when(is13)
    def _():
        z_b.start()

    for copy in core_copies:
        copy.wait_send()
    for k, copy in plane_copies:
        copy.wait_send()
    z_a.wait()

    @pl.when(is13)
    def _():
        z_b.wait()
        nb[c, x] = (zrecv[0].astype(F32) + zrecv[1].astype(F32)).astype(BF)

    @pl.when(jnp.logical_not(is13))
    def _():
        nb[c, x] = (acc[zh] + zrecv[1 - zh].astype(F32)).astype(BF)

    row_copies = []
    for d in range(1, 8):
        copy = remote(
            nb.at[c, x], nb.at[c, x], row_s.at[d - 1], row_r.at[d - 1], row_member(g, zh, y, x, c, d)
        )
        copy.start()
        row_copies.append(copy)
    for copy in row_copies:
        copy.wait()


def reduce_call(tcol, w):
    vm = pl.BlockSpec(memory_space=pltpu.VMEM)
    return pl.pallas_call(
        reduce_kernel,
        out_shape=jax.ShapeDtypeStruct((2, 4, 32, 640), BF),
        in_specs=[vm] * 2,
        out_specs=vm,
        scratch_shapes=[
            pltpu.VMEM((4, 256, 640), BF),
            pltpu.VMEM((4, 256, 640), BF),
            pltpu.VMEM((4, 4, 2, 32, 640), BF),
            pltpu.VMEM((15, 2, 32, 640), BF),
            pltpu.VMEM((2, 32, 640), F32),
            pltpu.VMEM((2, 32, 640), BF),
            pltpu.VMEM((2, 32, 640), BF),
            pltpu.SemaphoreType.DMA((4,)),
            pltpu.SemaphoreType.DMA((4,)),
            pltpu.SemaphoreType.DMA((15,)),
            pltpu.SemaphoreType.DMA((15,)),
            pltpu.SemaphoreType.DMA((2,)),
            pltpu.SemaphoreType.DMA((2,)),
            pltpu.SemaphoreType.DMA((7,)),
            pltpu.SemaphoreType.DMA((7,)),
        ],
        compiler_params=pltpu.CompilerParams(
            collective_id=1, has_side_effects=True, vmem_limit_bytes=VMEM_BYTES
        ),
        name="reduce_back",
    )(tcol, w)


def narrow_kernel(nb, mask, inj, wn, perm, pull, s_out, ig_out, nt, s_acc):
    j = lax.axis_index("mp") % 8
    fine = jnp.zeros((448, 320), F32)
    for i in range(2):
        for jj in range(2):
            spot = (2 * i + jj) * 128
            block = mm(nb[i], pull[jj]).astype(BF)
            fine = fine + mm(perm[:, spot : spot + 128], block)
    nt[...] = jnp.zeros_like(nt)
    nt[8:456, :] = fine * mask[...].astype(F32)
    pixel = lax.broadcasted_iota(jnp.int32, (392, 320), 0)
    column = pixel % 28
    rows = lax.broadcasted_iota(jnp.int32, (64, 392), 0)
    cols = lax.broadcasted_iota(jnp.int32, (64, 392), 1)
    mine = jnp.where((cols == rows + 49 * j) & (rows < 49), 1.0, 0.0).astype(BF)
    ig = jnp.zeros((64, 320), F32)
    s_acc[...] = jnp.zeros_like(s_acc)
    for t in range(9):
        dr, dc = 1 - t // 3, 1 - t % 3
        start = 8 + 28 + 28 * dr + dc
        moved = nt[start : start + 392, :]
        if dc == -1:
            moved = jnp.where(column >= 1, moved, 0.0)
        if dc == 1:
            moved = jnp.where(column <= 26, moved, 0.0)
        moved = moved.astype(BF)
        s_acc[40 * t : 40 * t + 40, :] = lax.dot_general(
            inj[...], moved, (((0,), (0,)), ((), ())), preferred_element_type=F32
        )
        own = mm(mine, moved).astype(BF)
        ig = ig + lax.dot_general(own, wn[t], (((1,), (1,)), ((), ())), preferred_element_type=F32)
    s_out[...] = s_acc[...].astype(BF)
    ig_out[...] = ig.astype(BF)


def pull():
    return spread().transpose(0, 2, 1)


def narrow_call(nb, mask, inj, wn):
    vm = pl.BlockSpec(memory_space=pltpu.VMEM)
    return pl.pallas_call(
        narrow_kernel,
        out_shape=(jax.ShapeDtypeStruct((384, 320), BF), jax.ShapeDtypeStruct((64, 320), BF)),
        in_specs=[vm] * 6,
        out_specs=(vm, vm),
        scratch_shapes=[pltpu.VMEM((464, 320), F32), pltpu.VMEM((384, 320), F32)],
        compiler_params=pltpu.CompilerParams(vmem_limit_bytes=VMEM_BYTES),
        name="narrow_local",
    )(nb, mask, inj, wn, jnp.asarray(fine_from_coarse(), BF), jnp.asarray(pull(), BF))


def holder(k):
    return (8 * k) // 3


def finish_kernel(
    s_in,
    wide,
    ng,
    wg,
    ybuf,
    zpart,
    zbuf,
    zfin,
    wbuf,
    w_s,
    w_r,
    y_s,
    y_r,
    z_s,
    z_r,
    b_s,
    b_r,
    pl_s,
    pl_r,
    co_s,
    co_r,
):
    g, zh, y, x, c = place()
    zz = zh * 8 + g
    j = 2 * x + c
    peer = device(g, zh, y, x, 1 - c)

    def along(d):
        other = (zz + d) % 16
        return device(other % 8, other // 8, y, x, c)

    barrier = pltpu.get_barrier_semaphore()
    for dy, dx in PLANE:
        greet(barrier, device(g, zh, (y + dy) % 4, (x + dx) % 4, c))
    for d in range(1, 16):
        greet(barrier, along(d))
    greet(barrier, peer)
    pl.semaphore_wait(barrier, 31)

    wide_copies = []
    for d in range(1, 8):
        gg = (g + d) % 8
        copy = remote(wide.at[gg], wbuf.at[d - 1], w_s.at[d - 1], w_r.at[d - 1], device(gg, zh, y, x, c))
        wide_copies.append(copy)

    y_copies = []
    for d in range(1, 4):
        yy = (y + d) % 4
        copy = remote(s_in.at[yy], ybuf.at[d - 1], y_s.at[d - 1], y_r.at[d - 1], device(g, zh, yy, x, c))
        copy.start()
        y_copies.append(copy)
    total = s_in[y].astype(F32)
    for copy, d in zip(y_copies, range(3)):
        copy.wait_recv()
        total = total + ybuf[d].astype(F32)
    zpart[...] = total.astype(BF)

    def z_copy(k, d):
        return remote(
            zpart.at[pl.ds(16 * k, 16)],
            zbuf.at[d - 1],
            z_s.at[k],
            z_r.at[d - 1],
            along(d),
        )

    for k in range(6):
        d = (holder(k) - zz + 16) % 16

        @pl.when(d != 0)
        def _():
            z_copy_to(zpart, zbuf, z_s, z_r, k, d, along).start()

    def back_copy(k, d):
        return remote(
            zfin.at[pl.ds(16 * k, 16)],
            zfin.at[pl.ds(16 * k, 16)],
            b_s.at[d - 1],
            b_r.at[k],
            along(d),
        )

    for k in range(6):

        @pl.when(zz == holder(k))
        def _():
            value = zpart[16 * k : 16 * k + 16, :].astype(F32)
            for d in range(1, 16):
                z_copy(k, d).wait_recv()
                value = value + zbuf[d - 1].astype(F32)
            zfin[16 * k : 16 * k + 16, :] = (value * (1.0 / 32.0)).astype(BF)
            for d in range(1, 16):
                back_copy(k, d).start()

    for copy in wide_copies:
        copy.start()

    for k in range(6):

        @pl.when(zz != holder(k))
        def _():
            back_copy(k, 1).wait_recv()

    plane_copies = []
    for k, (dy, dx) in enumerate(PLANE):
        copy = remote(
            zfin, ng.at[j, y], pl_s.at[k], pl_r.at[k], device(g, zh, (y + dy) % 4, (x + dx) % 4, c)
        )
        copy.start()
        plane_copies.append(copy)
    ng[j, y] = zfin[...]
    core_copies = []
    for k, (dy, dx) in enumerate([(0, 0)] + PLANE):
        if k > 0:
            plane_copies[k - 1].wait_recv()
        spot = ng.at[2 * ((x + 4 - dx) % 4) + c, (y + 4 - dy) % 4]
        copy = remote(spot, spot, co_s.at[k], co_r.at[k], peer)
        copy.start()
        core_copies.append(copy)

    terms = wide[g].astype(F32)
    for d in range(7):
        wide_copies[d].wait_recv()
        terms = terms + wbuf[d].astype(F32)
    wg[...] = (terms * (1.0 / 32.0)).astype(BF)

    for copy in y_copies + wide_copies + plane_copies:
        copy.wait_send()
    for k in range(6):

        @pl.when(zz != holder(k))
        def _():
            z_copy(k, 1).wait_send()

        @pl.when(zz == holder(k))
        def _():
            for d in range(1, 16):
                back_copy(k, d).wait_send()

    for copy in core_copies:
        copy.wait()


def z_copy_to(zpart, zbuf, z_s, z_r, k, d, along):
    return remote(zpart.at[pl.ds(16 * k, 16)], zbuf.at[d - 1], z_s.at[k], z_r.at[d - 1], along(d))


def finish_call(s, wide):
    vm = pl.BlockSpec(memory_space=pltpu.VMEM)
    dma = pltpu.SemaphoreType.DMA
    return pl.pallas_call(
        finish_kernel,
        out_shape=(
            jax.ShapeDtypeStruct((8, 4, 96, 320), BF),
            jax.ShapeDtypeStruct((160, 360), BF),
        ),
        in_specs=[vm] * 2,
        out_specs=(vm, vm),
        scratch_shapes=[
            pltpu.VMEM((3, 96, 320), BF),
            pltpu.VMEM((96, 320), BF),
            pltpu.VMEM((15, 16, 320), BF),
            pltpu.VMEM((96, 320), BF),
            pltpu.VMEM((7, 160, 360), BF),
            dma((7,)),
            dma((7,)),
            dma((3,)),
            dma((3,)),
            dma((6,)),
            dma((15,)),
            dma((15,)),
            dma((6,)),
            dma((15,)),
            dma((15,)),
            dma((16,)),
            dma((16,)),
        ],
        compiler_params=pltpu.CompilerParams(
            collective_id=2, has_side_effects=True, vmem_limit_bytes=VMEM_BYTES
        ),
        name="finish_sums",
    )(s, wide)


def tap_columns(tangent):
    padded = jnp.pad(tangent, ((0, 0), (1, 1), (1, 1), (0, 0)))
    taps = []
    for a in range(3):
        for b in range(3):
            taps.append(padded[:, 2 - a : 16 - a, 2 - b : 16 - b, :])
    cols = jnp.concatenate(taps, axis=3)
    pieces = []
    blank = jnp.zeros((16, 360), BF)
    for u in range(8):
        h = (u + 1) % 8
        image, half = h // 2, h % 2
        rim = 6 if half == 1 else 7
        pieces.append(cols[image, 7 * half : 7 * half + 7].reshape(98, 360))
        pieces.append(cols[image, rim])
        pieces.append(blank)
    stacked = jnp.concatenate(pieces, axis=0).reshape(2, 4, 4, 32, 360)
    return stacked.transpose(1, 2, 0, 3, 4).reshape(4, 256, 360)


def local(
    narrow_input, narrow_output, narrow_mask, wide_cotangent, wide_mask, narrow_weight, wide_weight
):
    g, zh, y, x, c = place()
    j = 2 * x + c
    stacked = jnp.stack([narrow_output, narrow_mask.astype(BF), narrow_input])
    blk = jnp.pad(stacked, ((0, 0), (0, 15), (0, 0)))
    gath, halo, xall = gather_call(blk)

    tangent = wide_cotangent * wide_mask.astype(BF)
    tcol = tap_columns(tangent)
    wmat = wide_weight.transpose(0, 1, 3, 2).reshape(360, 1280)
    nb = reduce_call(tcol, wmat).reshape(2, 128, 640)

    odd = y % 2 == 1
    zero = jnp.zeros((), BF)
    above = jnp.where(odd, zero, halo[21:49])
    below = jnp.where(odd, halo[0:28], zero)
    mask = jnp.concatenate([above, gath[:, 1, :49].reshape(392, 320), below], axis=0)
    rows = gath[:, 2, :49].reshape(392, 320)
    inj = lax.dynamic_slice_in_dim(rows, 40 * j, 40, 1)
    s, ig = narrow_call(nb, mask, inj, narrow_weight.reshape(9, 320, 320))

    wide = lax.dot_general(
        xall.reshape(2, 1024, 640),
        tcol.reshape(1024, 360),
        (((1,), (0,)), ((), ())),
        preferred_element_type=F32,
    )
    wide = wide.reshape(8, 160, 360).astype(BF)
    ng, wg = finish_call(s.reshape(4, 96, 320), wide)
    narrow_gradient = (
        ng.reshape(8, 384, 320)[:, :360].reshape(8, 9, 40, 320).transpose(1, 0, 2, 3).reshape(3, 3, 320, 320)
    )
    wide_gradient = wg.T.reshape(3, 3, 40, 160).transpose(0, 1, 3, 2)
    return (narrow_gradient, wide_gradient, ig[:49])


def solution(mesh):
    placed = (
        P(("dp", "mp"), None),
        P(("dp", "mp"), None),
        P(("dp", "mp"), None),
        P("dp", None, None, "mp"),
        P("dp", None, None, "mp"),
        P(),
        P(None, None, None, "mp"),
    )
    return jax.shard_map(
        local,
        mesh=mesh,
        in_specs=placed,
        out_specs=(P(), P(None, None, "dp", "mp"), P(("dp", "mp"), None)),
        check_vma=False,
    )
```
